32 devices in a mesh: groups: 2 (over x), expert: 16 (over z, y, core), dp: 1.
Axes of the slice: x: 2, y: 2, z: 4, core: 2. Of those that a mesh axis runs over, the one named last changes fastest.
Arguments:
- token_codes: bfloat16 [2048, 4096], P(('groups', 'expert', 'dp')), parts along dimension 0, may hold values from -6 to 6
- token_scales: bfloat16 [2048, 32], P(('groups', 'expert', 'dp')), parts along dimension 0, may hold values from 0.25 to 4
- expert_ids: int32 [2048, 8], P(('groups', 'expert', 'dp')), parts along dimension 0, may hold values from 0 to 15, all different within a row; in each aligned block of 64 rows (0 to 63, 64 to 127, ...) at most 48 rows name the same one
- gate_values: float32 [2048, 8], P(('groups', 'expert', 'dp')), parts along dimension 0, may hold values from 0.05 to 0.25
- w_gate: bfloat16 [16, 4096, 1536], P('expert', None, 'dp'), may hold values from -0.09375 to 0.09375
- w_up: bfloat16 [16, 4096, 1536], P('expert', None, 'dp'), may hold values from -0.09375 to 0.09375
- w_down: bfloat16 [16, 1536, 4096], P('expert', 'dp'), may hold values from -0.15625 to 0.15625
- gate_scales: float32 [16, 32, 12], P('expert', None, 'dp'), may hold values from 0.5 to 2
- up_scales: float32 [16, 32, 12], P('expert', None, 'dp'), may hold values from 0.5 to 2
- down_scales: float32 [16, 12, 32], P('expert', 'dp'), may hold values from 0.5 to 2
Outputs:
- mixed: bfloat16 [2048, 4096], P(('groups', 'expert', 'dp')), parts along dimension 0
The draws below stay inside these ranges and needn't reach their ends.
There are 2 independent parts, one for each index of `groups`. The reference program is written for one: setup_inputs(seed, part) draws one part's arguments, and reference() takes and returns one part's arrays. A program takes and returns all parts, laid end to end along the dimension named above; an argument that names none is the same for every part. Nothing has to cross between parts.
Inputs may be any that keep to these rules, and one draw needn't show every extreme that they name: `expert_ids`: each token names 8 different experts. Among the 64 tokens of one device no expert is named by more than 48 tokens, and in every draw some device names some expert in exactly 48 tokens.
All inputs are finite; a program needn't handle non-finite values.
Results may differ from the reference program's by a relative error of at most 0.028.
Values may be sent and summed in bfloat16 or wider, within the bound.
No kernel may reach another device: no remote copies, remote signals or barrier semaphores. Data moves between devices by JAX's collectives and lax.ppermute only.
A program may use at most 320 MiB of HBM per device.

```python
import math
import jax
import jax.numpy as jnp
import numpy as np
from jax import lax

D = 4096
FF = 1536
TOPK = 8
TOK_DEV = 64
EXPERTS = 16
CAP = 48
TOKENS = 1024
N_EXPERT = 16
N_DP = 1


def shard_levels(key, extent, cuts, low, top_value):
    level, own = 1.0, jax.random.fold_in(key, 6)
    for position, blocks in cuts:
        steps = jnp.exp(jax.random.uniform(jax.random.fold_in(own, position), (blocks,), jnp.float32, low / len(cuts), top_value / len(cuts)))
        level = level * jnp.repeat(steps, extent[position] // blocks).reshape([-1 if axis == position else 1 for axis in range(len(extent))])
    return level


def shared_out(stream_key, own, number, rows, amount, top, reach, skew):
    sequence = jax.random.permutation(stream_key, amount)
    crowded, ordinary = load_shares(amount, rows * top, reach, skew, True), load_shares(amount, rows * top, reach, skew, False)
    places = jnp.arange(amount)

    def named(tallies, rotation):
        used = int((tallies > 0).sum())
        fixed = max(1, used // 4)
        passed = fixed + (places - fixed + rotation * (used - fixed)) % max(1, amount - fixed)
        return jnp.zeros((amount,), jnp.int32).at[sequence[jnp.where(places < fixed, places, passed)]].set(jnp.asarray(tallies, jnp.int32))

    tallies = jnp.where(number % 4 == 0, named(crowded, number // 4), named(ordinary, number - number // 4 - 1))
    mixed = jax.random.permutation(jax.random.fold_in(own, 3), amount)
    donor, receiver = mixed[0:amount // 2 * 2:2], mixed[1:amount // 2 * 2:2]
    slack = jnp.minimum(tallies[donor] - 1, reach - tallies[receiver]) // 2
    slack = jnp.where((donor == sequence[0]) | (receiver == sequence[0]) | (tallies[receiver] == 0), 0, jnp.maximum(slack, 0))
    passed = jax.random.randint(jax.random.fold_in(own, 4), (amount // 2,), 0, 1 << 20) % (slack + 1)
    tallies = tallies.at[donor].add(-passed).at[receiver].add(passed)
    labels = jnp.searchsorted(jnp.cumsum(tallies), jnp.arange(rows * top), side="right").astype(jnp.int32)
    table = labels.reshape(top, rows).T
    table = table[jax.random.permutation(jax.random.fold_in(own, 1), rows)]
    rotation = jax.random.randint(jax.random.fold_in(own, 2), (rows, 1), 0, top)
    return jnp.take_along_axis(table, (jnp.arange(top)[None, :] + rotation) % top, axis=1)


def load_shares(amount, total, most, skew, full):
    weights = [(1 << 20) // math.isqrt(standing ** skew) + 1 for standing in range(1, amount + 1)]
    largest = most if full else min(most, max(-(-total // amount), total * weights[0] // sum(weights)))
    least = 1 if total - largest >= amount - 1 else 0
    given, surplus = [largest] + [least] * (amount - 1), total - largest - least * (amount - 1)
    while surplus > 0:
        free = [i for i in range(1, amount) if given[i] < largest] or [i for i in range(1, amount) if given[i] < most]
        pool, left = sum([weights[i] for i in free]), surplus
        for i in free:
            extra = min(most - given[i], max(1, left * weights[i] // pool), surplus)
            given[i] = given[i] + extra
            surplus = surplus - extra
    return np.array(given)


def noise(own_key, extent, width, reach, split=(), kind=jnp.bfloat16):
    factor_of = shard_levels(own_key, extent, split, -0.22, 0.18) if split else 1.0
    drawn = jax.random.normal(own_key, extent, jnp.float32) * width * factor_of
    return jnp.minimum(jnp.maximum(drawn, -reach), reach).astype(kind)


def setup_inputs(seed: int = 0, part: int = 0) -> dict:
    keys = jax.random.split(jax.random.key(seed), 11)
    part_splits = jax.random.split(jax.random.fold_in(keys[10], part), 11)
    token_codes = noise(part_splits[0], (TOKENS, D), 1.0, 6.0, ((0, 16),))
    token_scales = jnp.clip(jnp.exp(math.log(4.0) - 2.7725887 * jax.random.uniform(part_splits[1], (TOKENS, D // 128), jnp.float32) ** shard_levels(part_splits[1], (TOKENS, D // 128), ((0, 16),), -0.2, 0.2)), 0.25, 4.0).astype(jnp.bfloat16)
    expert_ids_keys = jax.random.split(jax.random.fold_in(part_splits[2], 1), TOKENS // TOK_DEV)
    expert_ids_turns = jax.random.permutation(jax.random.fold_in(part_splits[2], 3), TOKENS // TOK_DEV)
    expert_ids = jax.vmap(lambda own, number: shared_out(jax.random.fold_in(part_splits[2], 2), own, number, TOK_DEV, EXPERTS, TOPK, CAP, 2))(expert_ids_keys, expert_ids_turns).reshape((TOKENS, TOPK))
    gate_values = jnp.clip(0.05 + 0.2 * jax.random.uniform(part_splits[3], (TOKENS, TOPK), jnp.float32) ** shard_levels(part_splits[3], (TOKENS, TOPK), ((0, 16),), -0.2, 0.2), 0.05, 0.25)
    w_gate = noise(keys[4], (EXPERTS, D, FF), D ** -0.5, 0.09375, ((0, 16),))
    w_up = noise(keys[5], (EXPERTS, D, FF), D ** -0.5, 0.09375, ((0, 16),))
    w_down = noise(keys[6], (EXPERTS, FF, D), FF ** -0.5, 0.15625, ((0, 16),))
    gate_scales = jnp.clip(jnp.exp(math.log(2.0) - 1.3862944 * jax.random.uniform(keys[7], (EXPERTS, D // 128, FF // 128), jnp.float32) ** shard_levels(keys[7], (EXPERTS, D // 128, FF // 128), ((0, 16),), -0.2, 0.2)), 0.5, 2.0)
    up_scales = jnp.clip(jnp.exp(math.log(2.0) - 1.3862944 * jax.random.uniform(keys[8], (EXPERTS, D // 128, FF // 128), jnp.float32) ** shard_levels(keys[8], (EXPERTS, D // 128, FF // 128), ((0, 16),), -0.2, 0.2)), 0.5, 2.0)
    down_scales = jnp.clip(jnp.exp(math.log(2.0) - 1.3862944 * jax.random.uniform(keys[9], (EXPERTS, FF // 128, D // 128), jnp.float32) ** shard_levels(keys[9], (EXPERTS, FF // 128, D // 128), ((0, 16),), -0.2, 0.2)), 0.5, 2.0)
    return dict(token_codes=token_codes, token_scales=token_scales, expert_ids=expert_ids, gate_values=gate_values, w_gate=w_gate, w_up=w_up, w_down=w_down, gate_scales=gate_scales, up_scales=up_scales, down_scales=down_scales)


def dequant_rows(codes, scales):
    count = codes.shape[0]
    blocks = codes.astype(jnp.float32).reshape(count, scales.shape[1], 128) * scales.astype(jnp.float32)[:, :, None]
    return blocks.reshape(count, codes.shape[1]).astype(jnp.bfloat16)


def dequant_weight(weight, scales):
    height, breadth = weight.shape
    tiles = weight.astype(jnp.float32).reshape(height // 128, 128, breadth // 128, 128) * scales[:, None, :, None]
    return tiles.reshape(height, breadth).astype(jnp.bfloat16)


def reference(token_codes, token_scales, expert_ids, gate_values, w_gate, w_up, w_down, gate_scales, up_scales, down_scales):
    rows = dequant_rows(token_codes, token_scales)
    flat_ids = expert_ids.reshape(-1).astype(jnp.int32)
    flat_gates = gate_values.reshape(-1)
    order = jnp.argsort(flat_ids, stable=True).astype(jnp.int32)
    counts = jnp.sum((flat_ids[None, :] == jnp.arange(EXPERTS, dtype=jnp.int32)[:, None]).astype(jnp.int32), axis=1)
    starts = (jnp.cumsum(counts) - counts).astype(jnp.int32)
    limit = N_EXPERT * N_DP * CAP
    padded_order = jnp.concatenate([order, jnp.zeros((limit,), jnp.int32)])

    def one_expert(total, expert):
        index = lax.dynamic_slice_in_dim(padded_order, starts[expert], limit)
        live = jnp.arange(limit, dtype=jnp.int32) < counts[expert]
        chosen = rows[index // TOPK]
        gate_mat = dequant_weight(w_gate[expert], gate_scales[expert])
        up_mat = dequant_weight(w_up[expert], up_scales[expert])
        down_mat = dequant_weight(w_down[expert], down_scales[expert])
        gated = jnp.dot(chosen, gate_mat, preferred_element_type=jnp.float32)
        upward = jnp.dot(chosen, up_mat, preferred_element_type=jnp.float32)
        hidden = (jax.nn.silu(gated) * upward).astype(jnp.bfloat16)
        result = jnp.dot(hidden, down_mat, preferred_element_type=jnp.float32).astype(jnp.bfloat16)
        weight = jnp.where(live, flat_gates[index], jnp.float32(0.0))
        total = total.at[index // TOPK].add(weight[:, None] * result.astype(jnp.float32))
        return total, None

    start_total = jnp.zeros(token_codes.shape, jnp.float32)
    total, unused = lax.scan(one_expert, start_total, jnp.arange(EXPERTS, dtype=jnp.int32))
    return total.astype(jnp.bfloat16)
```

```python
import functools

import jax
import jax.numpy as jnp
from jax import lax
from jax.experimental import pallas as pl
from jax.experimental.pallas import tpu as pltpu
from jax.sharding import PartitionSpec as P

BF16 = jnp.bfloat16
F32 = jnp.float32
TILE_FF = 256
TILE_D = 512
MB = 1 << 20


def prep_kernel(codes_ref, scales_ref, ids_ref, gates_ref, first_ref, second_ref, *, experts):
    count, width = codes_ref.shape
    half = count // 2
    scales = scales_ref[...].astype(F32)
    for b in range(width // 128):
        columns = pl.ds(b * 128, 128)
        rows = (codes_ref[:, columns].astype(F32) * scales[:, b : b + 1]).astype(BF16)
        first_ref[:, columns] = rows[:half]
        second_ref[:, columns] = rows[half:]
    lane = lax.broadcasted_iota(jnp.int32, (count, 128), 1)
    expert = lane % experts
    dense = jnp.zeros((count, 128), F32)
    for k in range(ids_ref.shape[1]):
        dense = dense + jnp.where(ids_ref[:, k : k + 1] == expert, gates_ref[:, k : k + 1], 0.0)
    high = dense.astype(BF16).astype(F32)
    both = jnp.where(lane < experts, high, jnp.where(lane < 2 * experts, dense - high, 0.0)).astype(BF16)
    columns = pl.ds(width, 128)
    first_ref[:, columns] = both[:half]
    second_ref[:, columns] = both[half:]


def prep(codes, scales, ids, gates, experts):
    count, width = codes.shape
    shape = jax.ShapeDtypeStruct((count // 2, width + 128), BF16)
    return pl.pallas_call(
        functools.partial(prep_kernel, experts=experts),
        out_shape=(shape, shape),
        cost_estimate=pl.CostEstimate(flops=count * width, bytes_accessed=4 * count * width, transcendentals=0),
        name="prep",
    )(codes, scales, ids, gates)


def dequant_kernel(scales_ref, weight_ref, out_ref, *, tile):
    step = pl.program_id(0)
    height, breadth = weight_ref.shape
    for b in range(height // 128):
        for j in range(breadth // 128):
            scale = scales_ref[step * (height // 128) + b, j]
            block = weight_ref[pl.ds(b * 128, 128), pl.ds(j * 128, 128)].astype(F32) * scale
            out_ref[j * 128 // tile, pl.ds(b * 128, 128), pl.ds(j * 128 % tile, 128)] = block.astype(BF16)


def dequant(weight, scales, tile, name):
    height, breadth = weight.shape
    rows = 256 if breadth > 2048 else 512
    return pl.pallas_call(
        functools.partial(dequant_kernel, tile=tile),
        grid=(height // rows,),
        in_specs=[
            pl.BlockSpec(memory_space=pltpu.SMEM),
            pl.BlockSpec((rows, breadth), lambda i: (i, 0)),
        ],
        out_specs=pl.BlockSpec((breadth // tile, rows, tile), lambda i: (0, i, 0)),
        out_shape=jax.ShapeDtypeStruct((breadth // tile, height, tile), BF16),
        cost_estimate=pl.CostEstimate(flops=height * breadth, bytes_accessed=4 * height * breadth, transcendentals=0),
        compiler_params=pltpu.CompilerParams(vmem_limit_bytes=16 * MB),
        name=name,
    )(scales, weight)


def hidden_kernel(expert_ref, rows_ref, gate_ref, up_ref, hidden_ref, *, experts):
    width = gate_ref.shape[1]
    rows = rows_ref[:, :width]
    gated = jnp.dot(rows, gate_ref[0], preferred_element_type=F32)
    upward = jnp.dot(rows, up_ref[0], preferred_element_type=F32)
    sent = rows_ref[:, width:].astype(F32)
    lane = lax.broadcasted_iota(jnp.int32, sent.shape, 1)
    mine = expert_ref[0]
    value = jnp.sum(jnp.where((lane == mine) | (lane == mine + experts), sent, 0.0), axis=1, keepdims=True)
    hidden_ref[...] = (gated / (1.0 + jnp.exp(-gated)) * upward * value).astype(BF16)


def hidden_of(expert, rows, gate_mat, up_mat, experts):
    count = rows.shape[0]
    tiles, width, tile = gate_mat.shape
    return pl.pallas_call(
        functools.partial(hidden_kernel, experts=experts),
        grid=(tiles,),
        in_specs=[
            pl.BlockSpec(memory_space=pltpu.SMEM),
            pl.BlockSpec(rows.shape, lambda i: (0, 0)),
            pl.BlockSpec((1, width, tile), lambda i: (i, 0, 0)),
            pl.BlockSpec((1, width, tile), lambda i: (i, 0, 0)),
        ],
        out_specs=pl.BlockSpec((count, tile), lambda i: (0, i)),
        out_shape=jax.ShapeDtypeStruct((count, tiles * tile), BF16),
        cost_estimate=pl.CostEstimate(
            flops=4 * count * width * tiles * tile,
            bytes_accessed=4 * width * tiles * tile + 2 * count * width,
            transcendentals=count * tiles * tile,
        ),
        compiler_params=pltpu.CompilerParams(vmem_limit_bytes=40 * MB),
        name="hidden",
    )(expert, rows, gate_mat, up_mat)


def down_kernel(hidden_ref, down_ref, out_ref):
    out_ref[...] = jnp.dot(hidden_ref[...], down_ref[0], preferred_element_type=F32).astype(BF16)


def down_of(hidden, part, down_mat):
    count, depth = hidden.shape
    count //= 2
    tiles, _, tile = down_mat.shape
    return pl.pallas_call(
        down_kernel,
        grid=(tiles,),
        in_specs=[
            pl.BlockSpec((count, depth), lambda i: (part, 0)),
            pl.BlockSpec((1, depth, tile), lambda i: (i, 0, 0)),
        ],
        out_specs=pl.BlockSpec((count, tile), lambda i: (0, i)),
        out_shape=jax.ShapeDtypeStruct((count, tiles * tile), BF16),
        cost_estimate=pl.CostEstimate(
            flops=2 * count * depth * tiles * tile,
            bytes_accessed=2 * depth * tiles * tile + 2 * count * tiles * tile,
            transcendentals=0,
        ),
        compiler_params=pltpu.CompilerParams(vmem_limit_bytes=24 * MB),
        name="down",
    )(hidden, down_mat)


def total_of(*terms):
    return sum(t.astype(F32) for t in terms).astype(BF16)


def solution(mesh):
    experts, pairs = mesh.shape["expert"], mesh.shape["dp"]
    chips = experts * pairs // 2
    if pairs == 1:
        walk = [*range(0, chips, 2), *reversed(range(1, chips, 2))]
    else:
        walk = [*range(chips)]
    far = chips // 2
    names = ("expert", "dp")

    def shift(k):
        return [
            (2 * walk[p] + core, 2 * walk[(p + k) % chips] + core)
            for p in range(chips)
            for core in range(2)
        ]

    def right(a):
        return lax.ppermute(a, names, shift(1))

    def left(a):
        return lax.ppermute(a, names, shift(-1))

    def across(a):
        return lax.ppermute(a, names, [(i, i ^ 1) for i in range(2 * chips)])

    def gather(block):
        half = block.shape[0] // 2
        r = l = block
        own, other, held = [block], [], [block]
        for k in range(1, far):
            r, l = right(r), left(l)
            held += [r, l]
            other.append(across(jnp.concatenate(held)))
            own += [r, l]
            held = []
        last = jnp.concatenate([right(r[:half]), left(l[half:])])
        return jnp.concatenate([*own, last, *other, across(last)]), (r, l)

    def scatter(mine, theirs, block):
        half = block // 2

        def terms(k, side):
            if k == 0:
                at, size = 0, block
            elif k == far:
                at, size = (2 * far - 1) * block + side * half, half
            else:
                at, size = (2 * k - 1 + side) * block, block
            return mine[at : at + size], theirs[at : at + size]

        blank = jnp.zeros((half, mine.shape[1]), BF16)
        r = jnp.concatenate([blank, right(total_of(*terms(far, 1)))])
        l = jnp.concatenate([left(total_of(*terms(far, 0))), blank])
        for k in range(far - 1, 0, -1):
            r = right(total_of(r, *terms(k, 1)))
            l = left(total_of(l, *terms(k, 0)))
        return total_of(r, l, *terms(0, 0))

    def shards(codes, scales, ids, gates, w_gate, w_up, w_down, gate_scales, up_scales, down_scales):
        expert = lax.axis_index("expert").reshape(1)
        first, second = prep(codes, scales, ids, gates, experts)
        block = first.shape[0]
        rows1, seen = gather(first)
        second, _ = lax.optimization_barrier((second, seen))
        rows2, _ = gather(second)
        gate_mat = dequant(w_gate[0], gate_scales[0], TILE_FF, "dequant_gate")
        up_mat = dequant(w_up[0], up_scales[0], TILE_FF, "dequant_up")
        down_mat = dequant(w_down[0], down_scales[0], TILE_D, "dequant_down")
        outs = []
        for rows in (rows1, rows2):
            hidden = hidden_of(expert, rows, gate_mat, up_mat, experts)
            theirs = across(down_of(hidden, 1, down_mat))
            mine = down_of(hidden, 0, down_mat)
            outs.append(scatter(mine, theirs, block))
        return jnp.concatenate(outs)

    token = P(("groups", "expert", "dp"), None)
    return jax.shard_map(
        shards,
        mesh=mesh,
        in_specs=(
            token,
            token,
            token,
            token,
            P("expert", None, "dp"),
            P("expert", None, "dp"),
            P("expert", "dp", None),
            P("expert", None, "dp"),
            P("expert", None, "dp"),
            P("expert", "dp", None),
        ),
        out_specs=token,
        check_vma=False,
    )
```

```python
import functools

import jax
import jax.numpy as jnp
from jax import lax
from jax.experimental import pallas as pl
from jax.experimental.pallas import tpu as pltpu
from jax.sharding import PartitionSpec as P

BF16 = jnp.bfloat16
F32 = jnp.float32
TILE_FF = 256
TILE_D = 512
SLOT_BYTES = 5 << 20
PARTS_FF, PARTS_D = 3, 4
HID, DEQ = 3, 6
COST = 1024
MB = 1 << 20


def whole(space=pltpu.VMEM):
    return pl.BlockSpec(memory_space=space)


def ordered(kernel, operands, in_specs, out_shape, waits, *, holds=(), scratch=(), flops, moved, vmem, name):
    count, extra = len(operands), len(waits) + len(holds)

    def body(*refs):
        refs = [*refs[:count], *refs[count + extra :]]
        mark = refs.pop(count + len(out_shape))
        mark[...] = jnp.zeros_like(mark)
        kernel(*refs)

    return pl.pallas_call(
        body,
        in_specs=[*in_specs, *[whole(pl.ANY)] * len(waits), *[whole()] * len(holds)],
        out_specs=[whole()] * (len(out_shape) + 1),
        out_shape=[*out_shape, jax.ShapeDtypeStruct((8, 128), F32)],
        scratch_shapes=scratch,
        cost_estimate=pl.CostEstimate(flops=flops, bytes_accessed=moved, transcendentals=0),
        compiler_params=pltpu.CompilerParams(vmem_limit_bytes=vmem * MB),
        name=name,
    )(*operands, *waits, *holds)


def prep_kernel(codes_ref, scales_ref, ids_ref, gates_ref, out_ref, *, experts):
    count, width = codes_ref.shape
    scales = scales_ref[...].astype(F32).T
    for b in range(width // 128):
        columns = pl.ds(b * 128, 128)
        out_ref[:, columns] = (codes_ref[:, columns].astype(F32) * scales[:, b : b + 1]).astype(BF16)
    row = lax.broadcasted_iota(jnp.int32, (128, count), 0)
    expert = row % experts
    dense = jnp.zeros((128, count), F32)
    for k in range(ids_ref.shape[0]):
        dense = dense + jnp.where(ids_ref[k : k + 1, :] == expert, gates_ref[k : k + 1, :], 0.0)
    high = dense.astype(BF16).astype(F32)
    both = jnp.where(row < experts, high, jnp.where(row < 2 * experts, dense - high, 0.0))
    out_ref[:, pl.ds(width, 128)] = both.T.astype(BF16)


def prep(codes, scales, ids, gates, experts):
    count, width = codes.shape
    return pl.pallas_call(
        functools.partial(prep_kernel, experts=experts),
        in_specs=[whole()] * 4,
        out_specs=whole(),
        out_shape=pltpu.VMEM((count, width + 128), BF16),
        cost_estimate=pl.CostEstimate(flops=count * width, bytes_accessed=4 * count * width, transcendentals=0),
        name="prep",
    )(codes, scales.T, ids.T, gates.T)


def dequant_kernel(*refs, count, by_row, parts):
    all_scales, weights, refs = refs[:count], refs[count : 2 * count], refs[2 * count :]
    outs, slots, sems = refs[: count * parts], refs[count * parts : count * (parts + 1)], refs[count * (parts + 1) :]
    steps = weights[0].shape[0] // 128
    depth, _, breadth = slots[0].shape
    tiles, _, tile = outs[0].shape
    ahead = min(depth - 1, steps)

    def copy(m, i):
        slot = lax.rem(i, depth)
        source = weights[m].at[pl.ds(pl.multiple_of(i * 128, 128), 128)]
        return pltpu.make_async_copy(source, slots[m].at[slot], sems[m].at[slot])

    for i in range(ahead):
        for m in range(count):
            copy(m, i).start()

    @pl.loop(0, steps)
    def _(i):
        for m in range(count):

            @pl.when(i + ahead < steps)
            def _():
                copy(m, i + ahead).start()

            copy(m, i).wait()
            for j in range(breadth // 128):
                value = all_scales[m][i, 0, j] if by_row else all_scales[m][j, 0, i]
                block = slots[m][lax.rem(i, depth), :, pl.ds(j * 128, 128)].astype(F32) * value
                part, n = divmod(j * 128 // tile, tiles)
                at = pl.ds(pl.multiple_of(i * 128, 128), 128)
                outs[m * parts + part][n, at, pl.ds(j * 128 % tile, 128)] = block.astype(BF16)


def dequant(weights, scales, by_row, tile, parts, waits, name):
    count = len(weights)
    weights = [pltpu.with_memory_space_constraint(w, pltpu.HBM) for w in weights]
    height, breadth = weights[0].shape
    slots = max(2, min(SLOT_BYTES // (256 * breadth * count), height // 128))
    size = count * height * breadth
    *mats, mark = ordered(
        functools.partial(dequant_kernel, count=count, by_row=by_row, parts=parts),
        [*scales, *weights],
        [whole(pltpu.SMEM)] * count + [whole(pltpu.HBM)] * count,
        [pltpu.VMEM((breadth // tile // parts, height, tile), BF16)] * (count * parts),
        waits,
        scratch=[
            *[pltpu.VMEM((slots, 128, breadth), BF16)] * count,
            *[pltpu.SemaphoreType.DMA((slots,))] * count,
        ],
        flops=COST * size,
        moved=4 * size,
        vmem=DEQ,
        name=name,
    )
    return [mats[m * parts : (m + 1) * parts] for m in range(count)], mark


def hidden_kernel(*refs, experts, count):
    blocks, gates, ups = refs[: -2 * count - 2], refs[-2 * count - 2 : -count - 2], refs[-count - 2 : -2]
    hidden_ref, rows_ref = refs[-2:]
    tiles, width, tile = gates[0].shape
    at = 0
    for block in blocks:
        rows_ref[pl.ds(at, block.shape[0]), :] = block[...]
        at += block.shape[0]
    sent = rows_ref[:, pl.ds(width, 128)].astype(F32)
    lane = lax.broadcasted_iota(jnp.int32, sent.shape, 1)
    mine = lax.axis_index("expert")
    value = jnp.sum(jnp.where((lane == mine) | (lane == mine + experts), sent, 0.0), axis=1, keepdims=True)
    for i in range(count * tiles):
        part, n = divmod(i, tiles)
        rows = rows_ref[:, pl.ds(0, width)]
        gated = jnp.dot(rows, gates[part][n], preferred_element_type=F32)
        upward = jnp.dot(rows, ups[part][n], preferred_element_type=F32)
        hidden_ref[:, pl.ds(i * tile, tile)] = (gated / (1.0 + jnp.exp(-gated)) * upward * value).astype(BF16)


def hidden_of(blocks, gates, ups, experts, waits):
    rows = sum(b.shape[0] for b in blocks)
    tiles, width, tile = gates[0].shape
    depth = len(gates) * tiles * tile
    return ordered(
        functools.partial(hidden_kernel, experts=experts, count=len(gates)),
        [*blocks, *gates, *ups],
        [whole()] * (len(blocks) + 2 * len(gates)),
        [pltpu.VMEM((rows, depth), BF16)],
        waits,
        scratch=[pltpu.VMEM((rows, width + 128), BF16)],
        flops=2 * rows * width * depth,
        moved=2 * rows * width,
        vmem=HID,
        name="hidden",
    )


def down_kernel(hidden_ref, *refs):
    *mats, mine_ref, theirs_ref = refs
    tiles, _, tile = mats[0].shape
    half = mine_ref.shape[0]
    for i in range(len(mats) * tiles):
        part, n = divmod(i, tiles)
        out = jnp.dot(hidden_ref[...], mats[part][n], preferred_element_type=F32).astype(BF16)
        columns = pl.ds(i * tile, tile)
        mine_ref[:, columns] = out[:half]
        theirs_ref[:, columns] = out[half:]


def down_of(hidden, mats, waits):
    count, depth = hidden.shape
    tiles, _, tile = mats[0].shape
    width = len(mats) * tiles * tile
    return ordered(
        down_kernel,
        [hidden, *mats],
        [whole()] * (1 + len(mats)),
        [pltpu.VMEM((count // 2, width), BF16), jax.ShapeDtypeStruct((count // 2, width), BF16)],
        waits,
        flops=count * depth * width,
        moved=2 * count * width,
        vmem=1,
        name="down",
    )


def totals_kernel(*refs, plan):
    outs = refs[len(refs) - len(plan) :]
    for out, blocks in zip(outs, plan, strict=True):
        size = out.shape[0] // len(blocks)
        for n, terms in enumerate(blocks):
            total = sum(refs[i][pl.ds(at, size), :].astype(F32) for i, at in terms)
            out[pl.ds(n * size, size), :] = total.astype(BF16)


def totals(arrays, size, plan, waits=()):
    width = arrays[0].shape[1]
    rows = size * sum(map(len, plan))
    return ordered(
        functools.partial(totals_kernel, plan=plan),
        arrays,
        [whole()] * len(arrays),
        [jax.ShapeDtypeStruct((size * len(blocks), width), BF16) for blocks in plan],
        waits,
        flops=3 * rows * width,
        moved=8 * rows * width,
        vmem=1,
        name="totals",
    )


def after(value, mark):
    return lax.optimization_barrier((value, mark))


def solution(mesh):
    experts, pairs = mesh.shape["expert"], mesh.shape["dp"]
    chips = experts * pairs // 2
    if pairs == 1:
        walk = [*range(0, chips, 2), *reversed(range(1, chips, 2))]
    else:
        walk = [*range(chips)]
    far = chips // 2
    names = ("expert", "dp")

    def shift(k):
        return [
            (2 * walk[p] + core, 2 * walk[(p + k) % chips] + core)
            for p in range(chips)
            for core in range(2)
        ]

    def right(a):
        return lax.ppermute(a, names, shift(1))

    def left(a):
        return lax.ppermute(a, names, shift(-1))

    def across(a):
        return lax.ppermute(a, names, [(i, i ^ 1) for i in range(2 * chips)])

    def shards(codes, scales, ids, gates, w_gate, w_up, w_down, gate_scales, up_scales, down_scales):
        block = prep(codes, scales, ids, gates, experts)
        count = block.shape[0]
        half = count // 2

        l = left(block)
        r = right(block)
        home = [block, across(block)]
        (gate_mats, up_mats), mark = dequant(
            [w_gate[0], w_up[0]],
            [gate_scales.transpose(2, 0, 1), up_scales.transpose(2, 0, 1)],
            False,
            TILE_FF,
            PARTS_FF,
            [block],
            "dequant_both",
        )
        hiddens = []

        def hide(blocks, waits):
            hidden, mark = hidden_of(blocks, gate_mats, up_mats, experts, waits)
            hiddens.append(hidden)
            return mark

        for k in range(1, far + 1):
            (r, l), mark = after((r, l), mark)
            first, second = [((0, 0),), ((0, half),)], [((1, 0),), ((1, half),)]
            if k < far - 1:
                both, mark = totals([r, l], half, [[*first, *second]], [mark])
                l = left(l)
                r = right(r)
            elif k < far:
                r, l, both, mark = totals([r, l], half, [first[:1], second[1:], [*first, *second]], [mark])
                l = left(l)
                r = right(r)
            else:
                both, mark = totals([r, l], half, [[first[0], second[0]]], [mark])
            blocks = [both, across(both)]
            if k == 1:
                mark = hide(home, [mark])
            if k == min(2, far):
                (down_mats,), mark = dequant(
                    [w_down[0]],
                    [down_scales.transpose(1, 0, 2)],
                    True,
                    TILE_D,
                    PARTS_D,
                    [mark],
                    "dequant_down",
                )
            if k == far and far > 1:
                *upper, mark = down_of(hiddens[-1], down_mats, [mark])
            mark = hide(blocks, [mark])

        def down(k, waits):
            mine, theirs, mark = down_of(hiddens[k], down_mats, waits)
            return [mine, across(theirs)], mark

        def sums(pair, received, rows_r, rows_l, waits=()):
            own = [((0, at), (1, at)) for at in (rows_r, rows_l)]
            if received:
                own = [(*own[0], (2, 0)), (*own[1], (3, 0))]
            *both, mark = totals([*pair, *received], half, [[terms] for terms in own], waits)
            return both, mark

        def move(pair):
            return [right(pair[0]), left(pair[1])]

        short, pairs = [], {}
        if far > 1:
            pairs[far - 1] = [upper[0], across(upper[1])]
            short, mark = sums(pairs[far - 1], [], count, half)
            short = move(short)
        pairs[far], mark = down(far, [mark])
        long, mark = sums(pairs[far], [], half, 0)
        long = move(long)
        for k in range(far - 2, -1, -1):
            pairs[k], mark = down(k, [mark])
            if k > 0:
                short, mark = sums(pairs[k], short, count, half)
                short = move(short)
            long, mark = sums(pairs[k + 1], long, count + half, 0, [mark])
            long = move(long)
        arrays = [*pairs[0], *short, *long]
        if far > 1:
            plan = [((0, 0), (1, 0), (2, 0), (5, 0)), ((0, half), (1, half), (3, 0), (4, 0))]
        else:
            plan = [((0, 0), (1, 0), (3, 0)), ((0, half), (1, half), (2, 0))]
        return totals(arrays, half, [plan])[0]

    token = P(("groups", "expert", "dp"), None)
    return jax.shard_map(
        shards,
        mesh=mesh,
        in_specs=(
            token,
            token,
            token,
            token,
            P("expert", None, "dp"),
            P("expert", None, "dp"),
            P("expert", "dp", None),
            P("expert", None, "dp"),
            P("expert", None, "dp"),
            P("expert", "dp", None),
        ),
        out_specs=token,
        check_vma=False,
    )
```

```python
import functools

import jax
import jax.numpy as jnp
from jax import lax
from jax.experimental import pallas as pl
from jax.experimental.pallas import tpu as pltpu
from jax.sharding import PartitionSpec as P

BF16 = jnp.bfloat16
F32 = jnp.float32
TILE_FF = 256
TILE_D = 512
SLOT_BYTES = 5 << 20
PARTS_FF, PARTS_D = 2, 4
HID, DEQ = 3, 6
COST = 1024
MB = 1 << 20


def whole(space=pltpu.VMEM):
    return pl.BlockSpec(memory_space=space)


def ordered(kernel, operands, in_specs, out_shape, waits, *, holds=(), scratch=(), flops, moved, vmem, name):
    count, extra = len(operands), len(waits) + len(holds)

    def body(*refs):
        refs = [*refs[:count], *refs[count + extra :]]
        mark = refs.pop(count + len(out_shape))
        mark[...] = jnp.zeros_like(mark)
        kernel(*refs)

    return pl.pallas_call(
        body,
        in_specs=[*in_specs, *[whole(pl.ANY)] * len(waits), *[whole()] * len(holds)],
        out_specs=[whole()] * (len(out_shape) + 1),
        out_shape=[*out_shape, jax.ShapeDtypeStruct((8, 128), F32)],
        scratch_shapes=scratch,
        cost_estimate=pl.CostEstimate(flops=flops, bytes_accessed=moved, transcendentals=0),
        compiler_params=pltpu.CompilerParams(vmem_limit_bytes=vmem * MB),
        name=name,
    )(*operands, *waits, *holds)


def prep_kernel(codes_ref, scales_ref, ids_ref, gates_ref, out_ref, *, experts):
    count, width = codes_ref.shape
    scales = scales_ref[...].astype(F32).T
    for b in range(width // 128):
        columns = pl.ds(b * 128, 128)
        out_ref[:, columns] = (codes_ref[:, columns].astype(F32) * scales[:, b : b + 1]).astype(BF16)
    row = lax.broadcasted_iota(jnp.int32, (128, count), 0)
    expert = row % experts
    dense = jnp.zeros((128, count), F32)
    for k in range(ids_ref.shape[0]):
        dense = dense + jnp.where(ids_ref[k : k + 1, :] == expert, gates_ref[k : k + 1, :], 0.0)
    high = dense.astype(BF16).astype(F32)
    both = jnp.where(row < experts, high, jnp.where(row < 2 * experts, dense - high, 0.0))
    out_ref[:, pl.ds(width, 128)] = both.T.astype(BF16)


def prep(codes, scales, ids, gates, experts):
    count, width = codes.shape
    return pl.pallas_call(
        functools.partial(prep_kernel, experts=experts),
        in_specs=[whole()] * 4,
        out_specs=whole(),
        out_shape=pltpu.VMEM((count, width + 128), BF16),
        cost_estimate=pl.CostEstimate(flops=count * width, bytes_accessed=4 * count * width, transcendentals=0),
        name="prep",
    )(codes, scales.T, ids.T, gates.T)


def dequant_kernel(*refs, count, by_row, parts):
    all_scales, weights, refs = refs[:count], refs[count : 2 * count], refs[2 * count :]
    outs, slots, sems = refs[: count * parts], refs[count * parts : count * (parts + 1)], refs[count * (parts + 1) :]
    steps = weights[0].shape[0] // 128
    depth, _, breadth = slots[0].shape
    tiles, _, tile = outs[0].shape
    ahead = min(depth - 1, steps)

    def copy(m, i):
        slot = lax.rem(i, depth)
        source = weights[m].at[pl.ds(pl.multiple_of(i * 128, 128), 128)]
        return pltpu.make_async_copy(source, slots[m].at[slot], sems[m].at[slot])

    for i in range(ahead):
        for m in range(count):
            copy(m, i).start()

    @pl.loop(0, steps)
    def _(i):
        for m in range(count):

            @pl.when(i + ahead < steps)
            def _():
                copy(m, i + ahead).start()

            copy(m, i).wait()
            for j in range(breadth // 128):
                value = all_scales[m][i, 0, j] if by_row else all_scales[m][j, 0, i]
                block = slots[m][lax.rem(i, depth), :, pl.ds(j * 128, 128)].astype(F32) * value
                part, n = divmod(j * 128 // tile, tiles)
                at = pl.ds(pl.multiple_of(i * 128, 128), 128)
                outs[m * parts + part][n, at, pl.ds(j * 128 % tile, 128)] = block.astype(BF16)


def dequant(weights, scales, by_row, tile, parts, waits, name):
    count = len(weights)
    weights = [pltpu.with_memory_space_constraint(w, pltpu.HBM) for w in weights]
    height, breadth = weights[0].shape
    slots = max(2, min(SLOT_BYTES // (256 * breadth * count), height // 128))
    size = count * height * breadth
    while breadth // tile % parts:
        parts -= 1
    *mats, mark = ordered(
        functools.partial(dequant_kernel, count=count, by_row=by_row, parts=parts),
        [*scales, *weights],
        [whole(pltpu.SMEM)] * count + [whole(pltpu.HBM)] * count,
        [pltpu.VMEM((breadth // tile // parts, height, tile), BF16)] * (count * parts),
        waits,
        scratch=[
            *[pltpu.VMEM((slots, 128, breadth), BF16)] * count,
            *[pltpu.SemaphoreType.DMA((slots,))] * count,
        ],
        flops=COST * size,
        moved=4 * size,
        vmem=DEQ,
        name=name,
    )
    return [mats[m * parts : (m + 1) * parts] for m in range(count)], mark


def hidden_kernel(*refs, experts, count):
    blocks, gates, ups = refs[: -2 * count - 2], refs[-2 * count - 2 : -count - 2], refs[-count - 2 : -2]
    hidden_ref, rows_ref = refs[-2:]
    tiles, width, tile = gates[0].shape
    at = 0
    for block in blocks:
        rows_ref[pl.ds(at, block.shape[0]), :] = block[...]
        at += block.shape[0]
    sent = rows_ref[:, pl.ds(width, 128)].astype(F32)
    lane = lax.broadcasted_iota(jnp.int32, sent.shape, 1)
    mine = lax.axis_index("expert")
    value = jnp.sum(jnp.where((lane == mine) | (lane == mine + experts), sent, 0.0), axis=1, keepdims=True)

    @pl.loop(0, tiles)
    def _(n):
        for part in range(count):
            rows = rows_ref[:, pl.ds(0, width)]
            gated = jnp.dot(rows, gates[part][n], preferred_element_type=F32)
            upward = jnp.dot(rows, ups[part][n], preferred_element_type=F32)
            columns = pl.ds(pl.multiple_of((part * tiles + n) * tile, tile), tile)
            hidden_ref[:, columns] = (gated / (1.0 + jnp.exp(-gated)) * upward * value).astype(BF16)


def hidden_of(blocks, gates, ups, experts, waits, name):
    rows = sum(b.shape[0] for b in blocks)
    tiles, width, tile = gates[0].shape
    depth = len(gates) * tiles * tile
    return ordered(
        functools.partial(hidden_kernel, experts=experts, count=len(gates)),
        [*blocks, *gates, *ups],
        [whole()] * (len(blocks) + 2 * len(gates)),
        [pltpu.VMEM((rows, depth), BF16)],
        waits,
        scratch=[pltpu.VMEM((rows, width + 128), BF16)],
        flops=2 * rows * width * depth,
        moved=2 * rows * width,
        vmem=HID,
        name=name,
    )


def down_kernel(hidden_ref, *refs):
    *mats, mine_ref, theirs_ref = refs
    tiles, _, tile = mats[0].shape
    half = mine_ref.shape[0]

    @pl.loop(0, tiles)
    def _(n):
        for part in range(len(mats)):
            out = jnp.dot(hidden_ref[...], mats[part][n], preferred_element_type=F32).astype(BF16)
            columns = pl.ds(pl.multiple_of((part * tiles + n) * tile, tile), tile)
            mine_ref[:, columns] = out[:half]
            theirs_ref[:, columns] = out[half:]


def down_of(hidden, mats, waits, name):
    count, depth = hidden.shape
    tiles, _, tile = mats[0].shape
    width = len(mats) * tiles * tile
    return ordered(
        down_kernel,
        [hidden, *mats],
        [whole()] * (1 + len(mats)),
        [pltpu.VMEM((count // 2, width), BF16), jax.ShapeDtypeStruct((count // 2, width), BF16)],
        waits,
        flops=1,
        moved=1,
        vmem=1,
        name=name,
    )


def totals_kernel(*refs, plan):
    outs = refs[len(refs) - len(plan) :]
    for out, blocks in zip(outs, plan, strict=True):
        size = out.shape[0] // len(blocks)
        for n, terms in enumerate(blocks):
            total = sum(refs[i][pl.ds(at, size), :].astype(F32) for i, at in terms)
            out[pl.ds(n * size, size), :] = total.astype(BF16)


def totals(arrays, size, plan, waits=(), name="totals"):
    width = arrays[0].shape[1]
    rows = size * sum(map(len, plan))
    return ordered(
        functools.partial(totals_kernel, plan=plan),
        arrays,
        [whole()] * len(arrays),
        [jax.ShapeDtypeStruct((size * len(blocks), width), BF16) for blocks in plan],
        waits,
        flops=1,
        moved=1,
        vmem=1,
        name=name,
    )


def after(value, mark):
    return lax.optimization_barrier((value, mark))


def solution(mesh):
    experts, pairs = mesh.shape["expert"], mesh.shape["dp"]
    chips = experts * pairs // 2
    if pairs == 1:
        walk = [*range(0, chips, 2), *reversed(range(1, chips, 2))]
    else:
        walk = [*range(chips)]
    far = chips // 2
    names = ("expert", "dp")

    def shift(k):
        return [
            (2 * walk[p] + core, 2 * walk[(p + k) % chips] + core)
            for p in range(chips)
            for core in range(2)
        ]

    def right(a):
        return lax.ppermute(a, names, shift(1))

    def left(a):
        return lax.ppermute(a, names, shift(-1))

    def across(a):
        return lax.ppermute(a, names, [(i, i ^ 1) for i in range(2 * chips)])

    def shards(codes, scales, ids, gates, w_gate, w_up, w_down, gate_scales, up_scales, down_scales):
        block = prep(codes, scales, ids, gates, experts)
        count = block.shape[0]
        half = count // 2

        l = left(block)
        r = right(block)
        home = [block, across(block)]
        (gate_mats, up_mats), mark = dequant(
            [w_gate[0], w_up[0]],
            [gate_scales.transpose(2, 0, 1), up_scales.transpose(2, 0, 1)],
            False,
            TILE_FF,
            PARTS_FF,
            [block],
            "dequant_both",
        )
        hiddens = []

        def hide(blocks, waits):
            hidden, mark = hidden_of(blocks, gate_mats, up_mats, experts, waits, f"H{len(hiddens)}")
            hiddens.append(hidden)
            return mark

        for k in range(1, far + 1):
            (r, l), mark = after((r, l), mark)
            first, second = [((0, 0),), ((0, half),)], [((1, 0),), ((1, half),)]
            if k < far - 1:
                both, mark = totals([r, l], half, [[*first, *second]], [mark])
                l = left(l)
                r = right(r)
            elif k < far:
                r, l, both, mark = totals([r, l], half, [first[:1], second[1:], [*first, *second]], [mark])
                l = left(l)
                r = right(r)
            else:
                both, mark = totals([r, l], half, [[first[0], second[0]]], [mark])
            blocks = [both, across(both)]
            if k == 1:
                mark = hide(home, [mark])
            if k == min(2, far):
                (down_mats,), mark = dequant(
                    [w_down[0]],
                    [down_scales.transpose(1, 0, 2)],
                    True,
                    TILE_D,
                    PARTS_D,
                    [mark],
                    "dequant_down",
                )
            if k == far:
                *upper, mark = down_of(hiddens[-1], down_mats, [mark], f"D{k - 1}")
            mark = hide(blocks, [mark])

        def down(k, waits):
            mine, theirs, mark = down_of(hiddens[k], down_mats, waits, f"D{k}")
            return [mine, across(theirs)], mark

        def sums(name, pair, received, rows_r, rows_l, waits=()):
            own = [((0, at), (1, at)) for at in (rows_r, rows_l)]
            if received:
                own = [(*own[0], (2, 0)), (*own[1], (3, 0))]
            *both, mark = totals([*pair, *received], half, [[terms] for terms in own], waits, name)
            return both, mark

        def move(pair):
            return [right(pair[0]), left(pair[1])]

        pairs = {far - 1: [upper[0], across(upper[1])]}
        short, mark = sums(f"S{far - 1}", pairs[far - 1], [], count, half)
        short = move(short)
        pairs[far], mark = down(far, [mark])
        for k in range(far - 2, -1, -1):
            pairs[k], mark = down(k, [mark])
        long = []
        for k in range(far - 2, -1, -1):
            at = (count + half, 0) if long else (half, 0)
            long, mark = sums(f"L{k + 2}", pairs[k + 2], long, *at, [mark])
            long = move(long)
            if k > 0:
                short, mark = sums(f"S{k}", pairs[k], short, count, half, [mark])
                short = move(short)
        long, _ = sums("L1", pairs[1], long, count + half, 0, [mark])
        long = move(long)
        arrays = [*pairs[0], *short, *long]
        plan = [((0, 0), (1, 0), (2, 0), (5, 0)), ((0, half), (1, half), (3, 0), (4, 0))]
        return totals(arrays, half, [plan])[0]

    token = P(("groups", "expert", "dp"), None)
    return jax.shard_map(
        shards,
        mesh=mesh,
        in_specs=(
            token,
            token,
            token,
            token,
            P("expert", None, "dp"),
            P("expert", None, "dp"),
            P("expert", "dp", None),
            P("expert", None, "dp"),
            P("expert", None, "dp"),
            P("expert", "dp", None),
        ),
        out_specs=token,
        check_vma=False,
    )
```

```python
import functools

import jax
import jax.numpy as jnp
from jax import lax
from jax.experimental import pallas as pl
from jax.experimental.pallas import tpu as pltpu
from jax.sharding import PartitionSpec as P

BF16 = jnp.bfloat16
F32 = jnp.float32
TILE_FF = 256
TILE_D = 512
SLOT_BYTES = 5 << 20
PARTS_FF, PARTS_D = 3, 4
HID, DEQ = 3, 6
COST = 1024
MB = 1 << 20


def whole(space=pltpu.VMEM):
    return pl.BlockSpec(memory_space=space)


def ordered(kernel, operands, in_specs, out_shape, waits, *, holds=(), scratch=(), flops, moved, vmem, name):
    count, extra = len(operands), len(waits) + len(holds)

    def body(*refs):
        refs = [*refs[:count], *refs[count + extra :]]
        mark = refs.pop(count + len(out_shape))
        mark[...] = jnp.zeros_like(mark)
        kernel(*refs)

    return pl.pallas_call(
        body,
        in_specs=[*in_specs, *[whole(pl.ANY)] * len(waits), *[whole()] * len(holds)],
        out_specs=[whole()] * (len(out_shape) + 1),
        out_shape=[*out_shape, jax.ShapeDtypeStruct((8, 128), F32)],
        scratch_shapes=scratch,
        cost_estimate=pl.CostEstimate(flops=flops, bytes_accessed=moved, transcendentals=0),
        compiler_params=pltpu.CompilerParams(vmem_limit_bytes=vmem * MB),
        name=name,
    )(*operands, *waits, *holds)


def prep_kernel(codes_ref, scales_ref, ids_ref, gates_ref, out_ref, *, experts):
    count, width = codes_ref.shape
    scales = scales_ref[...].astype(F32).T
    for b in range(width // 128):
        columns = pl.ds(b * 128, 128)
        out_ref[:, columns] = (codes_ref[:, columns].astype(F32) * scales[:, b : b + 1]).astype(BF16)
    row = lax.broadcasted_iota(jnp.int32, (128, count), 0)
    expert = row % experts
    dense = jnp.zeros((128, count), F32)
    for k in range(ids_ref.shape[0]):
        dense = dense + jnp.where(ids_ref[k : k + 1, :] == expert, gates_ref[k : k + 1, :], 0.0)
    high = dense.astype(BF16).astype(F32)
    both = jnp.where(row < experts, high, jnp.where(row < 2 * experts, dense - high, 0.0))
    out_ref[:, pl.ds(width, 128)] = both.T.astype(BF16)


def prep(codes, scales, ids, gates, experts):
    count, width = codes.shape
    return pl.pallas_call(
        functools.partial(prep_kernel, experts=experts),
        in_specs=[whole()] * 4,
        out_specs=whole(),
        out_shape=pltpu.VMEM((count, width + 128), BF16),
        cost_estimate=pl.CostEstimate(flops=count * width, bytes_accessed=4 * count * width, transcendentals=0),
        name="prep",
    )(codes, scales.T, ids.T, gates.T)


def dequant_kernel(*refs, count, by_row, parts):
    all_scales, weights, refs = refs[:count], refs[count : 2 * count], refs[2 * count :]
    outs, slots, sems = refs[: count * parts], refs[count * parts : count * (parts + 1)], refs[count * (parts + 1) :]
    steps = weights[0].shape[0] // 128
    depth, _, breadth = slots[0].shape
    tiles, _, tile = outs[0].shape
    ahead = min(depth - 1, steps)

    def copy(m, i):
        slot = lax.rem(i, depth)
        source = weights[m].at[pl.ds(pl.multiple_of(i * 128, 128), 128)]
        return pltpu.make_async_copy(source, slots[m].at[slot], sems[m].at[slot])

    for i in range(ahead):
        for m in range(count):
            copy(m, i).start()

    @pl.loop(0, steps)
    def _(i):
        for m in range(count):

            @pl.when(i + ahead < steps)
            def _():
                copy(m, i + ahead).start()

            copy(m, i).wait()
            for j in range(breadth // 128):
                value = all_scales[m][i, 0, j] if by_row else all_scales[m][j, 0, i]
                block = slots[m][lax.rem(i, depth), :, pl.ds(j * 128, 128)].astype(F32) * value
                part, n = divmod(j * 128 // tile, tiles)
                at = pl.ds(pl.multiple_of(i * 128, 128), 128)
                outs[m * parts + part][n, at, pl.ds(j * 128 % tile, 128)] = block.astype(BF16)


def dequant(weights, scales, by_row, tile, parts, waits, name):
    count = len(weights)
    weights = [pltpu.with_memory_space_constraint(w, pltpu.HBM) for w in weights]
    height, breadth = weights[0].shape
    slots = max(2, min(SLOT_BYTES // (256 * breadth * count), height // 128))
    size = count * height * breadth
    while breadth // tile % parts:
        parts -= 1
    *mats, mark = ordered(
        functools.partial(dequant_kernel, count=count, by_row=by_row, parts=parts),
        [*scales, *weights],
        [whole(pltpu.SMEM)] * count + [whole(pltpu.HBM)] * count,
        [pltpu.VMEM((breadth // tile // parts, height, tile), BF16)] * (count * parts),
        waits,
        scratch=[
            *[pltpu.VMEM((slots, 128, breadth), BF16)] * count,
            *[pltpu.SemaphoreType.DMA((slots,))] * count,
        ],
        flops=COST * size,
        moved=4 * size,
        vmem=DEQ,
        name=name,
    )
    return [mats[m * parts : (m + 1) * parts] for m in range(count)], mark


def hidden_kernel(*refs, experts, count):
    blocks, gates, ups = refs[: -2 * count - 2], refs[-2 * count - 2 : -count - 2], refs[-count - 2 : -2]
    hidden_ref, rows_ref = refs[-2:]
    tiles, width, tile = gates[0].shape
    at = 0
    for block in blocks:
        rows_ref[pl.ds(at, block.shape[0]), :] = block[...]
        at += block.shape[0]
    sent = rows_ref[:, pl.ds(width, 128)].astype(F32)
    lane = lax.broadcasted_iota(jnp.int32, sent.shape, 1)
    mine = lax.axis_index("expert")
    value = jnp.sum(jnp.where((lane == mine) | (lane == mine + experts), sent, 0.0), axis=1, keepdims=True)

    @pl.loop(0, tiles)
    def _(n):
        for part in range(count):
            rows = rows_ref[:, pl.ds(0, width)]
            gated = jnp.dot(rows, gates[part][n], preferred_element_type=F32)
            upward = jnp.dot(rows, ups[part][n], preferred_element_type=F32)
            columns = pl.ds(pl.multiple_of((part * tiles + n) * tile, tile), tile)
            hidden_ref[:, columns] = (gated / (1.0 + jnp.exp(-gated)) * upward * value).astype(BF16)


def hidden_of(blocks, gates, ups, experts, waits, name):
    rows = sum(b.shape[0] for b in blocks)
    tiles, width, tile = gates[0].shape
    depth = len(gates) * tiles * tile
    return ordered(
        functools.partial(hidden_kernel, experts=experts, count=len(gates)),
        [*blocks, *gates, *ups],
        [whole()] * (len(blocks) + 2 * len(gates)),
        [pltpu.VMEM((rows, depth), BF16)],
        waits,
        scratch=[pltpu.VMEM((rows, width + 128), BF16)],
        flops=16 * rows * width * depth,
        moved=2 * rows * width,
        vmem=HID,
        name=name,
    )


def down_kernel(hidden_ref, *refs):
    *mats, mine_ref, theirs_ref = refs
    tiles, _, tile = mats[0].shape
    half = mine_ref.shape[0]

    @pl.loop(0, tiles)
    def _(n):
        for part in range(len(mats)):
            out = jnp.dot(hidden_ref[...], mats[part][n], preferred_element_type=F32).astype(BF16)
            columns = pl.ds(pl.multiple_of((part * tiles + n) * tile, tile), tile)
            mine_ref[:, columns] = out[:half]
            theirs_ref[:, columns] = out[half:]


def down_of(hidden, mats, waits, name):
    count, depth = hidden.shape
    tiles, _, tile = mats[0].shape
    width = len(mats) * tiles * tile
    return ordered(
        down_kernel,
        [hidden, *mats],
        [whole()] * (1 + len(mats)),
        [pltpu.VMEM((count // 2, width), BF16), jax.ShapeDtypeStruct((count // 2, width), BF16)],
        waits,
        flops=8 * count * depth * width,
        moved=1,
        vmem=1,
        name=name,
    )


def totals_kernel(*refs, plan):
    outs = refs[len(refs) - len(plan) :]
    for out, blocks in zip(outs, plan, strict=True):
        size = out.shape[0] // len(blocks)
        for n, terms in enumerate(blocks):
            total = sum(refs[i][pl.ds(at, size), :].astype(F32) for i, at in terms)
            out[pl.ds(n * size, size), :] = total.astype(BF16)


def totals(arrays, size, plan, waits=(), name="totals"):
    width = arrays[0].shape[1]
    rows = size * sum(map(len, plan))
    return ordered(
        functools.partial(totals_kernel, plan=plan),
        arrays,
        [whole()] * len(arrays),
        [jax.ShapeDtypeStruct((size * len(blocks), width), BF16) for blocks in plan],
        waits,
        flops=1,
        moved=1,
        vmem=1,
        name=name,
    )


def after(value, mark):
    return lax.optimization_barrier((value, mark))


def solution(mesh):
    experts, pairs = mesh.shape["expert"], mesh.shape["dp"]
    chips = experts * pairs // 2
    if pairs == 1:
        walk = [*range(0, chips, 2), *reversed(range(1, chips, 2))]
    else:
        walk = [*range(chips)]
    far = chips // 2
    names = ("expert", "dp")

    def shift(k):
        return [
            (2 * walk[p] + core, 2 * walk[(p + k) % chips] + core)
            for p in range(chips)
            for core in range(2)
        ]

    def right(a):
        return lax.ppermute(a, names, shift(1))

    def left(a):
        return lax.ppermute(a, names, shift(-1))

    def across(a):
        return lax.ppermute(a, names, [(i, i ^ 1) for i in range(2 * chips)])

    def shards(codes, scales, ids, gates, w_gate, w_up, w_down, gate_scales, up_scales, down_scales):
        block = prep(codes, scales, ids, gates, experts)
        count = block.shape[0]
        half = count // 2

        l = left(block)
        r = right(block)
        home = [block, across(block)]
        (gate_mats, up_mats), mark = dequant(
            [w_gate[0], w_up[0]],
            [gate_scales.transpose(2, 0, 1), up_scales.transpose(2, 0, 1)],
            False,
            TILE_FF,
            PARTS_FF,
            [block],
            "dequant_both",
        )
        hiddens = []

        def hide(blocks, waits):
            hidden, mark = hidden_of(blocks, gate_mats, up_mats, experts, waits, f"H{len(hiddens)}")
            hiddens.append(hidden)
            return mark

        for k in range(1, far + 1):
            (r, l), mark = after((r, l), mark)
            first, second = [((0, 0),), ((0, half),)], [((1, 0),), ((1, half),)]
            if k < far - 1:
                both, mark = totals([r, l], half, [[*first, *second]], [mark])
                l = left(l)
                r = right(r)
            elif k < far:
                r, l, both, mark = totals([r, l], half, [first[:1], second[1:], [*first, *second]], [mark])
                l = left(l)
                r = right(r)
            else:
                both, mark = totals([r, l], half, [[first[0], second[0]]], [mark])
            blocks = [both, across(both)]
            if k == 1:
                mark = hide(home, [mark])
            if k == min(2, far):
                (down_mats,), mark = dequant(
                    [w_down[0]],
                    [down_scales.transpose(1, 0, 2)],
                    True,
                    TILE_D,
                    PARTS_D,
                    [mark],
                    "dequant_down",
                )
            if k == far:
                *upper, mark = down_of(hiddens[-1], down_mats, [mark], f"D{k - 1}")
            mark = hide(blocks, [mark])

        def down(k, waits):
            mine, theirs, mark = down_of(hiddens[k], down_mats, waits, f"D{k}")
            return [mine, across(theirs)], mark

        def sums(name, pair, received, rows_r, rows_l, waits=()):
            own = [((0, at), (1, at)) for at in (rows_r, rows_l)]
            if received:
                own = [(*own[0], (2, 0)), (*own[1], (3, 0))]
            *both, mark = totals([*pair, *received], half, [[terms] for terms in own], waits, name)
            return both, mark

        def move(pair):
            return [right(pair[0]), left(pair[1])]

        pairs = {far - 1: [upper[0], across(upper[1])]}
        short, mark = sums(f"S{far - 1}", pairs[far - 1], [], count, half)
        short = move(short)
        pairs[far], mark = down(far, [mark])
        for k in range(far - 2, -1, -1):
            pairs[k], mark = down(k, [mark])
        long = []
        for k in range(far - 2, -1, -1):
            at = (count + half, 0) if long else (half, 0)
            long, mark = sums(f"L{k + 2}", pairs[k + 2], long, *at, [mark])
            long = move(long)
            if k > 0:
                short, mark = sums(f"S{k}", pairs[k], short, count, half, [mark])
                short = move(short)
        long, _ = sums("L1", pairs[1], long, count + half, 0, [mark])
        long = move(long)
        arrays = [*pairs[0], *short, *long]
        plan = [((0, 0), (1, 0), (2, 0), (5, 0)), ((0, half), (1, half), (3, 0), (4, 0))]
        return totals(arrays, half, [plan])[0]

    token = P(("groups", "expert", "dp"), None)
    return jax.shard_map(
        shards,
        mesh=mesh,
        in_specs=(
            token,
            token,
            token,
            token,
            P("expert", None, "dp"),
            P("expert", None, "dp"),
            P("expert", "dp", None),
            P("expert", None, "dp"),
            P("expert", None, "dp"),
            P("expert", "dp", None),
        ),
        out_specs=token,
        check_vma=False,
    )
```
